32 devices in a mesh: row: 16 (over z, y, x), col: 2 (over core).
Axes of the slice: x: 2, y: 2, z: 4, core: 2. Of those that a mesh axis runs over, the one named last changes fastest.
Arguments:
- basis: bfloat16 [128, 64, 512], P('row', 'col'), may hold values from -0.25 to 0.25
- positions: float32 [128, 3, 512], P('row'), may hold values from 0 to 1
- seglen: float32 [128, 512], P('row'), may hold values from 0.5 to 2
- radius: float32 [128, 512], P('row'), may hold values from 0.05 to 0.2
- neighbours: int32 [128, 16], P('row'), may hold values from 0 to 127, as said below
- counts: int32 [128], P('row'), may hold values from 1 to 16, as said below
Outputs:
- reduced: float32 [128, 64, 1024], P('row', 'col')
The draws below stay inside these ranges and needn't reach their ends.
Inputs may be any that keep to these rules, and one draw needn't show every extreme that they name: `neighbours`: each neighbour index differs from its own block's index by at most 8; slot 0 always differs by exactly 8. `counts`: the first block of every 8 has all 16 slots live.
All inputs are finite; a program needn't handle non-finite values.
Results may differ from the reference program's by a relative error of at most 0.019.
Values may be sent and summed in bfloat16 or wider, within the bound.
A program may use at most 64 MiB of HBM per device.

```python
import math
import jax
import jax.numpy as jnp
from jax import lax

UNK = 512
NB = 64
NEAR = 16
BLK_DEV = 8
BLOCKS = 128


def draw_neighbours(key, part):
    first_key = jax.random.fold_in(key, 11)
    sign_key = jax.random.fold_in(key, 12)
    offsets = jax.random.randint(first_key, (BLOCKS, NEAR), -BLK_DEV, BLK_DEV + 1)
    signs = jax.random.randint(sign_key, (BLOCKS,), 0, 2) * 2 - 1
    offsets = offsets.at[:, 0].set(signs * BLK_DEV)
    own = jnp.arange(BLOCKS, dtype=jnp.int32)[:, None]
    forward = own + offsets
    mirrored = own - offsets
    outside = (forward < 0) | (forward >= BLOCKS)
    return jnp.where(outside, mirrored, forward).astype(jnp.int32)


def draw_counts(key, part):
    low_key = jax.random.fold_in(key, 21)
    each_key = jax.random.fold_in(key, 22)
    lowest = jax.random.randint(low_key, (BLOCKS // BLK_DEV, 1), 1, NEAR // 2 + 2)
    drawn = jax.random.randint(each_key, (BLOCKS // BLK_DEV, BLK_DEV), 0, 1 << 20)
    spread = NEAR + 1 - lowest
    values = lowest + drawn % spread
    values = values.at[:, 0].set(NEAR)
    return values.reshape(BLOCKS).astype(jnp.int32)


def steps_of(rng, extent, split, smallest, largest):
    loudness = 1.0
    for dim, parts in split:
        draws = jax.random.uniform(jax.random.fold_in(jax.random.fold_in(rng, 6), dim), (parts,), jnp.float32, smallest / len(split), largest / len(split))
        loudness = loudness * jnp.repeat(jnp.exp(draws), extent[dim] // parts).reshape((-1,) + (1,) * (len(extent) - 1 - dim))
    return loudness


def centred(stream_key, shape, scale, limit, shards=(), kind=jnp.bfloat16):
    entries = scale * jax.random.normal(stream_key, shape, jnp.float32)
    if shards:
        entries = entries * steps_of(stream_key, shape, shards, -0.22, 0.18)
    return jnp.clip(entries, -limit, limit).astype(kind)


def setup_inputs(seed: int = 0) -> dict:
    key_of = jax.random.split(jax.random.key(seed), 7)
    return {
        "basis": centred(key_of[0], (BLOCKS, NB, UNK), UNK ** -0.5, 0.25, ((0, 16), (1, 2))),
        "positions": jnp.clip(1.0 * jax.random.uniform(key_of[1], (BLOCKS, 3, UNK), jnp.float32) ** steps_of(key_of[1], (BLOCKS, 3, UNK), ((0, 16),), -0.2, 0.2), 0.0, 1.0),
        "seglen": jnp.clip(jnp.exp(math.log(2.0) - 1.3862944 * jax.random.uniform(key_of[2], (BLOCKS, UNK), jnp.float32) ** steps_of(key_of[2], (BLOCKS, UNK), ((0, 16),), -0.2, 0.2)), 0.5, 2.0),
        "radius": jnp.clip(jnp.exp(math.log(0.2) - 1.3862944 * jax.random.uniform(key_of[3], (BLOCKS, UNK), jnp.float32) ** steps_of(key_of[3], (BLOCKS, UNK), ((0, 16),), -0.2, 0.2)), 0.05, 0.2),
        "neighbours": draw_neighbours(jax.random.fold_in(key_of[6], 71), 0),
        "counts": draw_counts(jax.random.fold_in(key_of[6], 71), 0),
    }


def reference(basis, positions, seglen, radius, neighbours, counts):

    def one_block(items):
        own_basis, own_pos, own_len, own_rad, near_ids, live_count = items
        pos_near = jnp.take(positions, near_ids, axis=0)
        len_near = jnp.take(seglen, near_ids, axis=0)
        rad_near = jnp.take(radius, near_ids, axis=0)
        dist_sq = jnp.zeros((near_ids.shape[0], own_pos.shape[1], own_pos.shape[1]), jnp.float32)
        for coord in range(3):
            gap = own_pos[coord][None, :, None] - pos_near[:, coord][:, None, :]
            dist_sq = dist_sq + gap * gap
        coupling = own_len[None, :, None] * len_near[:, None, :] / jnp.sqrt(dist_sq + own_rad[None, :, None] * rad_near[:, None, :])
        coupling = coupling.astype(jnp.bfloat16)
        left = jnp.einsum('pm,kmn->kpn', own_basis.astype(jnp.float32), coupling.astype(jnp.float32)).astype(jnp.bfloat16)
        panels = jnp.take(basis, near_ids, axis=0)
        tiles = jnp.einsum('kpn,kqn->pkq', left.astype(jnp.float32), panels.astype(jnp.float32))
        live = (jnp.arange(near_ids.shape[0], dtype=jnp.int32) < live_count).astype(jnp.float32)
        tiles = tiles * live[None, :, None]
        return tiles.reshape(tiles.shape[0], -1)
    return lax.map(one_block, (basis, positions, seglen, radius, neighbours, counts))
```

```python
import functools

import jax
import jax.numpy as jnp
from jax import lax
from jax.experimental import pallas as pl
from jax.experimental.pallas import tpu as pltpu
from jax.sharding import PartitionSpec as P

F32 = jnp.float32
BF16 = jnp.bfloat16
MESH = pl.DeviceIdType.MESH
VMEM = pl.BlockSpec(memory_space=pltpu.VMEM)
SMEM = pl.BlockSpec(memory_space=pltpu.SMEM)
NT = (((1,), (1,)), ((), ()))


def gather_kernel(rows, basis, pos, length, rad, own_p, halo_p, own_g, halo_g,
                  mine, core_s, px_s, px_r, fw_s, fw_r, g_s, g_r, core_r):
    r, c = lax.axis_index("row"), lax.axis_index("col")
    blks, half, unk = basis.shape
    pairs = blks // 2
    other = 1 - c
    odd = r % 2
    partner = r + 1 - 2 * odd
    ahead = r + 2 - 4 * odd
    behind = r - 2 + 4 * odd
    has_ahead = jnp.logical_and(ahead >= 0, ahead < rows)
    has_behind = jnp.logical_and(behind >= 0, behind < rows)
    got = 1 - odd
    relayed = odd

    barrier = pltpu.get_barrier_semaphore()
    pl.semaphore_signal(barrier, inc=1, device_id=(r, other), device_id_type=MESH)
    pl.semaphore_signal(barrier, inc=1, device_id=(partner, c), device_id_type=MESH)
    pl.semaphore_signal(barrier, inc=1, device_id=(partner, other), device_id_type=MESH)

    @pl.when(has_ahead)
    def _():
        pl.semaphore_signal(barrier, inc=1, device_id=(ahead, c), device_id_type=MESH)

    @pl.when(has_behind)
    def _():
        pl.semaphore_signal(barrier, inc=1, device_id=(behind, c), device_id_type=MESH)

    for i in range(blks):
        q, a = i % 2, i // 2
        scaled = (basis[i].astype(F32) * length[i:i + 1]).astype(BF16)
        mine[q, a] = scaled
        own_g[q, 4 * a:4 * a + 3] = pos[i]
        own_g[q, 4 * a + 3:4 * a + 4] = rad[i:i + 1]

    pl.semaphore_wait(barrier, 3 + has_ahead.astype(jnp.int32) + has_behind.astype(jnp.int32))

    here = pl.ds(pl.multiple_of(half * c, half), half)
    there = pl.ds(pl.multiple_of(half * other, half), half)

    def to_partner(core, k):
        return pltpu.make_async_remote_copy(
            src_ref=mine.at[core], dst_ref=halo_p.at[1 - got, :, here],
            send_sem=px_s.at[k], recv_sem=px_r.at[k], device_id=(partner, core), device_id_type=MESH)

    same = to_partner(c, 0)
    cross = to_partner(other, 1)
    geo = pltpu.make_async_remote_copy(
        src_ref=own_g.at[c], dst_ref=halo_g.at[1 - got], send_sem=g_s.at[0], recv_sem=g_r.at[0],
        device_id=(partner, c), device_id_type=MESH)
    core = pltpu.make_async_remote_copy(
        src_ref=mine, dst_ref=own_p.at[:, :, here], send_sem=core_s, recv_sem=core_r,
        device_id=(r, other), device_id_type=MESH)
    same.start()
    cross.start()
    geo.start()
    core.start()
    own_p[:, :, here] = mine[...]

    def forward(place, k):
        return pltpu.make_async_remote_copy(
            src_ref=halo_p.at[got, :, place], dst_ref=halo_p.at[relayed, :, place],
            send_sem=fw_s.at[k], recv_sem=fw_r.at[k], device_id=(ahead, c), device_id_type=MESH)

    fw_geo = pltpu.make_async_remote_copy(
        src_ref=halo_g.at[got], dst_ref=halo_g.at[relayed], send_sem=g_s.at[1], recv_sem=g_r.at[1],
        device_id=(ahead, c), device_id_type=MESH)
    first, second = forward(here, 0), forward(there, 1)
    same.wait_recv()

    @pl.when(has_ahead)
    def _():
        first.start()

    cross.wait_recv()

    @pl.when(has_ahead)
    def _():
        second.start()

    geo.wait_recv()

    @pl.when(has_ahead)
    def _():
        fw_geo.start()

    core.wait()
    same.wait_send()
    cross.wait_send()
    geo.wait_send()

    @pl.when(has_ahead)
    def _():
        first.wait_send()
        second.wait_send()
        fw_geo.wait_send()

    @pl.when(has_behind)
    def _():
        first.wait_recv()
        second.wait_recv()
        fw_geo.wait_recv()


def tile_kernel(near, counts, me, own_p, halo_p, own_g, halo_g, tiles,
                seen, todo_b, todo_j, todo_s, cols, rows_t, panels_t, c0, c1, parts):
    blks, slots = near.shape
    pairs = blks // 2
    unk = own_p.shape[-1]
    first_block, c = me[0], me[1]
    per = blks + 1

    def clear(i, _):
        seen[i] = 0
        return 0

    lax.fori_loop(0, blks * per, clear, 0)

    def per_block(b, n):
        def per_slot(k, n):
            j = near[b, k] - first_block + blks
            slot = b * per + (j - b) // 2
            take = jnp.logical_and(j % 2 == c, seen[slot] == 0)

            @pl.when(take)
            def _():
                seen[slot] = 1
                todo_b[n] = b
                todo_j[n] = j // 2
                todo_s[n] = (b % pairs) * per + (j - b) // 2

            return n + take.astype(jnp.int32)

        return lax.fori_loop(0, counts[b], per_slot, n)

    todo_b[0] = 0
    todo_j[0] = pairs
    todo_s[0] = pairs * per
    n = lax.fori_loop(0, blks, per_block, 1)
    for extra in range(3):
        todo_b[n + extra] = 0
        todo_j[n + extra] = pairs
        todo_s[n + extra] = pairs * per

    def lay_down(b, _):
        for x in range(4):
            row = own_g[b % 2, pl.ds((b // 2) * 4 + x, 1)]
            cols[b, x] = jnp.transpose(jnp.broadcast_to(row, (128, unk)))
        return 0

    lax.fori_loop(0, blks, lay_down, 0)
    rows_t[0] = halo_g[0]
    rows_t[1] = own_g[c]
    rows_t[2] = halo_g[1]

    def lay_panels(a, _):
        for side, panel in ((0, halo_p[0, a]), (1, own_p[c, a]), (2, halo_p[1, a])):
            panels_t[side * pairs + a] = jnp.transpose(jnp.concatenate([panel, panel], axis=0))
        return 0

    lax.fori_loop(0, pairs, lay_panels, 0)

    lane = lax.broadcasted_iota(jnp.int32, (own_p.shape[2], 128), 1)

    def couple(t, into):
        b, j = todo_b[t], todo_j[t]
        side, a = j // pairs, j % pairs
        near_rows = [rows_t[side, pl.ds(a * 4 + x, 1)] for x in range(4)]
        step = 64
        for m in range(0, unk, step):
            mine = [cols[b, x, m:m + step] for x in range(4)]
            for q in range(0, unk, 128):
                dist = mine[3] * near_rows[3][:, q:q + 128]
                for x in range(3):
                    gap = mine[x] - near_rows[x][:, q:q + 128]
                    dist = dist + gap * gap
                into[m:m + step, q:q + 128] = lax.rsqrt(dist).astype(BF16)

    def contract(t, c_ref):
        b, j, s = todo_b[t], todo_j[t], todo_s[t]
        left = jnp.dot(own_p[b % 2, b // 2], c_ref[...], preferred_element_type=F32)
        tile = jnp.dot(left.astype(BF16), panels_t[j], preferred_element_type=F32)
        upper = b // pairs
        parts[s] = jnp.where((lane >= 64) == (upper == 1), tile, parts[s])

    def steps(i, _):
        t = 2 * i
        couple(t + 1, c1)
        contract(t, c0)
        couple(t + 2, c0)
        contract(t + 1, c1)
        return 0

    lax.fori_loop(0, (n + 1) // 2, steps, 0)
    tiles[...] = parts[0:tiles.shape[0]].astype(tiles.dtype)


def place_kernel(near, counts, tiles, out, both, s_sem, r_sem):
    r, c = lax.axis_index("row"), lax.axis_index("col")
    blks, slots = near.shape
    pairs = blks // 2
    per = blks + 1
    half = out.shape[1]
    other = 1 - c
    barrier = pltpu.get_barrier_semaphore()
    pl.semaphore_signal(barrier, inc=1, device_id=(r, other), device_id_type=MESH)
    pl.semaphore_wait(barrier, 1)
    copy = pltpu.make_async_remote_copy(
        src_ref=tiles.at[:, pl.ds(pl.multiple_of(half * other, half), half)], dst_ref=both.at[c],
        send_sem=s_sem, recv_sem=r_sem, device_id=(r, other), device_id_type=MESH)
    copy.start()
    both[c] = tiles[:, pl.ds(pl.multiple_of(half * c, half), half)]
    copy.wait()
    first_block = r * blks
    for b in range(blks):
        up = b // pairs

        def one(k):
            j = near[b, k] - first_block + blks
            near_at = jnp.clip((j - b) // 2, 0, per - 1)
            tile = both[j % 2, (b % pairs) * per + near_at].astype(F32)
            tile = tile[:, 64 * up:64 * up + 64]
            return jnp.where(k < counts[b], tile, 0.0)

        for k in range(0, slots, 2):
            out[b, :, 64 * k:64 * k + 128] = jnp.concatenate([one(k), one(k + 1)], axis=1)


def on_device(rows, basis, positions, seglen, radius, neighbours, counts):
    blks, half, unk = basis.shape
    pairs = blks // 2
    per = blks + 1
    full = 2 * half
    slots = neighbours.shape[1]
    dma = pltpu.SemaphoreType.DMA
    own_p, halo_p, own_g, halo_g = pl.pallas_call(
        functools.partial(gather_kernel, rows),
        out_shape=(
            jax.ShapeDtypeStruct((2, pairs, full, unk), BF16),
            jax.ShapeDtypeStruct((2, pairs, full, unk), BF16),
            jax.ShapeDtypeStruct((2, 4 * pairs, unk), F32),
            jax.ShapeDtypeStruct((2, 4 * pairs, unk), F32),
        ),
        in_specs=[VMEM] * 4,
        out_specs=(VMEM,) * 4,
        scratch_shapes=[pltpu.VMEM((2, pairs, half, unk), BF16), dma, dma((2,)), dma((2,)), dma((2,)),
                        dma((2,)), dma((2,)), dma((2,)), dma],
        compiler_params=pltpu.CompilerParams(
            collective_id=0, has_side_effects=True, vmem_limit_bytes=24 << 20),
    )(basis, positions, seglen, radius)

    me = jnp.stack([lax.axis_index("row") * blks, lax.axis_index("col")]).astype(jnp.int32)
    tiles = pl.pallas_call(
        tile_kernel,
        out_shape=jax.ShapeDtypeStruct((pairs * per, full, 128), BF16),
        in_specs=[SMEM] * 3 + [VMEM] * 4,
        out_specs=VMEM,
        scratch_shapes=[
            pltpu.SMEM((blks * per,), jnp.int32),
            pltpu.SMEM((blks * slots + 8,), jnp.int32),
            pltpu.SMEM((blks * slots + 8,), jnp.int32),
            pltpu.SMEM((blks * slots + 8,), jnp.int32),
            pltpu.VMEM((blks, 4, unk, 128), F32),
            pltpu.VMEM((3, 4 * pairs, unk), F32),
            pltpu.VMEM((3 * pairs, unk, 128), BF16),
            pltpu.VMEM((unk, unk), BF16),
            pltpu.VMEM((unk, unk), BF16),
            pltpu.VMEM((pairs * per + 1, full, 128), F32),
        ],
        compiler_params=pltpu.CompilerParams(vmem_limit_bytes=40 << 20),
    )(neighbours, counts, me, own_p, halo_p, own_g, halo_g)

    return pl.pallas_call(
        place_kernel,
        out_shape=jax.ShapeDtypeStruct((blks, half, 64 * slots), F32),
        in_specs=[SMEM] * 2 + [VMEM],
        out_specs=VMEM,
        scratch_shapes=[pltpu.VMEM((2, pairs * per, half, 128), BF16),
                        dma, dma],
        compiler_params=pltpu.CompilerParams(
            collective_id=1, has_side_effects=True, vmem_limit_bytes=24 << 20),
    )(neighbours, counts, tiles)


def solution(mesh):
    placed = (
        P("row", "col", None),
        P("row", None, None),
        P("row", None),
        P("row", None),
        P("row", None),
        P("row"),
    )
    return jax.shard_map(
        functools.partial(on_device, mesh.shape["row"]),
        mesh=mesh, in_specs=placed, out_specs=P("row", "col", None), check_vma=False
    )
```

```python
import functools

import jax
import jax.numpy as jnp
from jax import lax
from jax.experimental import pallas as pl
from jax.experimental.pallas import tpu as pltpu
from jax.sharding import PartitionSpec as P

F32 = jnp.float32
BF16 = jnp.bfloat16
MESH = pl.DeviceIdType.MESH
VMEM = pl.BlockSpec(memory_space=pltpu.VMEM)
SMEM = pl.BlockSpec(memory_space=pltpu.SMEM)
NT = (((1,), (1,)), ((), ()))


def gather_kernel(rows, basis, pos, length, rad, own_p, halo_p, own_g, halo_g,
                  mine, core_s, px_s, px_r, fw_s, fw_r, g_s, g_r, core_r):
    r, c = lax.axis_index("row"), lax.axis_index("col")
    blks, half, unk = basis.shape
    pairs = blks // 2
    other = 1 - c
    odd = r % 2
    partner = r + 1 - 2 * odd
    ahead = r + 2 - 4 * odd
    behind = r - 2 + 4 * odd
    has_ahead = jnp.logical_and(ahead >= 0, ahead < rows)
    has_behind = jnp.logical_and(behind >= 0, behind < rows)
    got = 1 - odd
    relayed = odd

    barrier = pltpu.get_barrier_semaphore()
    pl.semaphore_signal(barrier, inc=1, device_id=(r, other), device_id_type=MESH)
    pl.semaphore_signal(barrier, inc=1, device_id=(partner, c), device_id_type=MESH)
    pl.semaphore_signal(barrier, inc=1, device_id=(partner, other), device_id_type=MESH)

    @pl.when(has_ahead)
    def _():
        pl.semaphore_signal(barrier, inc=1, device_id=(ahead, c), device_id_type=MESH)

    @pl.when(has_behind)
    def _():
        pl.semaphore_signal(barrier, inc=1, device_id=(behind, c), device_id_type=MESH)

    for i in range(blks):
        q, a = i % 2, i // 2
        scaled = (basis[i].astype(F32) * length[i:i + 1]).astype(BF16)
        mine[q, a] = scaled
        own_g[q, 4 * a:4 * a + 3] = pos[i]
        own_g[q, 4 * a + 3:4 * a + 4] = rad[i:i + 1]

    pl.semaphore_wait(barrier, 3 + has_ahead.astype(jnp.int32) + has_behind.astype(jnp.int32))

    here = pl.ds(pl.multiple_of(half * c, half), half)
    there = pl.ds(pl.multiple_of(half * other, half), half)

    def to_partner(core, k):
        return pltpu.make_async_remote_copy(
            src_ref=mine.at[core], dst_ref=halo_p.at[1 - got, :, here],
            send_sem=px_s.at[k], recv_sem=px_r.at[k], device_id=(partner, core), device_id_type=MESH)

    same = to_partner(c, 0)
    cross = to_partner(other, 1)
    geo = pltpu.make_async_remote_copy(
        src_ref=own_g.at[c], dst_ref=halo_g.at[1 - got], send_sem=g_s.at[0], recv_sem=g_r.at[0],
        device_id=(partner, c), device_id_type=MESH)
    core = pltpu.make_async_remote_copy(
        src_ref=mine, dst_ref=own_p.at[:, :, here], send_sem=core_s, recv_sem=core_r,
        device_id=(r, other), device_id_type=MESH)
    same.start()
    cross.start()
    geo.start()
    core.start()
    own_p[:, :, here] = mine[...]

    def forward(place, k):
        return pltpu.make_async_remote_copy(
            src_ref=halo_p.at[got, :, place], dst_ref=halo_p.at[relayed, :, place],
            send_sem=fw_s.at[k], recv_sem=fw_r.at[k], device_id=(ahead, c), device_id_type=MESH)

    fw_geo = pltpu.make_async_remote_copy(
        src_ref=halo_g.at[got], dst_ref=halo_g.at[relayed], send_sem=g_s.at[1], recv_sem=g_r.at[1],
        device_id=(ahead, c), device_id_type=MESH)
    first, second = forward(here, 0), forward(there, 1)
    same.wait_recv()

    @pl.when(has_ahead)
    def _():
        first.start()

    cross.wait_recv()

    @pl.when(has_ahead)
    def _():
        second.start()

    geo.wait_recv()

    @pl.when(has_ahead)
    def _():
        fw_geo.start()

    core.wait()
    same.wait_send()
    cross.wait_send()
    geo.wait_send()

    @pl.when(has_ahead)
    def _():
        first.wait_send()
        second.wait_send()
        fw_geo.wait_send()

    @pl.when(has_behind)
    def _():
        first.wait_recv()
        second.wait_recv()
        fw_geo.wait_recv()


def tile_kernel(near, counts, me, own_p, halo_p, own_g, halo_g, tiles,
                seen, todo_b, todo_j, todo_s, own_f, near_f, panels_t, c0, c1, l0, l1, parts):
    blks, slots = near.shape
    pairs = blks // 2
    unk = own_p.shape[-1]
    first_block, c = me[0], me[1]
    per = blks + 1

    def clear(i, _):
        seen[i] = 0
        return 0

    lax.fori_loop(0, blks * per, clear, 0)

    def per_block(b, n):
        def per_slot(k, n):
            j = near[b, k] - first_block + blks
            slot = b * per + (j - b) // 2
            take = jnp.logical_and(j % 2 == c, seen[slot] == 0)

            @pl.when(take)
            def _():
                seen[slot] = 1
                todo_b[n] = b
                todo_j[n] = j // 2
                todo_s[n] = (b % pairs) * per + (j - b) // 2

            return n + take.astype(jnp.int32)

        return lax.fori_loop(0, counts[b], per_slot, n)

    for first in range(2):
        todo_b[first] = 0
        todo_j[first] = pairs
        todo_s[first] = pairs * per
    n = lax.fori_loop(0, blks, per_block, 2)
    for extra in range(3):
        todo_b[n + extra] = 0
        todo_j[n + extra] = pairs
        todo_s[n + extra] = pairs * per

    def split(v):
        high = v.astype(BF16).astype(F32)
        return high, v - high

    def features(geo, a, lhs):
        one = jnp.ones((1, unk), F32)
        norm = jnp.zeros((1, unk), F32)
        out = []
        for x in range(4):
            v = geo[4 * a + x:4 * a + x + 1]
            high, low = split(v if x == 3 else v - 0.5)
            low = low.astype(BF16).astype(F32)
            whole = high + low
            if x < 3:
                norm = norm + whole * whole
            if lhs:
                scale = 1.0 if x == 3 else -2.0
                out += [scale * high, scale * high, scale * low, scale * low]
            else:
                out += [high, low, high, low]
        n0, rest = split(norm)
        n1, n2 = split(rest)
        out += [n0, n1, n2, one, one, one] if lhs else [one, one, one, n0, n1, n2]
        out.append(jnp.zeros((feats - len(out), unk), F32))
        return jnp.concatenate(out, axis=0)

    feats = near_f.shape[1]
    for b in range(blks):
        own_f[b] = jnp.transpose(features(own_g[b % 2], b // 2, True)).astype(BF16)
    for a in range(pairs):
        near_f[a] = features(halo_g[0], a, False).astype(BF16)
        near_f[pairs + a] = features(own_g[c], a, False).astype(BF16)
        near_f[2 * pairs + a] = features(halo_g[1], a, False).astype(BF16)

    def lay_panels(a, _):
        for side, panel in ((0, halo_p[0, a]), (1, own_p[c, a]), (2, halo_p[1, a])):
            panels_t[side * pairs + a] = jnp.transpose(jnp.concatenate([panel, panel], axis=0))
        return 0

    lax.fori_loop(0, pairs, lay_panels, 0)

    lane = lax.broadcasted_iota(jnp.int32, (own_p.shape[2], 128), 1)

    def couple(t, into):
        dist = jnp.dot(own_f[todo_b[t]], near_f[todo_j[t]], preferred_element_type=F32)
        into[...] = lax.rsqrt(dist).astype(BF16)

    def reduce_own(t, c_ref, left):
        b = todo_b[t]
        left[...] = jnp.dot(
            own_p[b % 2, b // 2], c_ref[...], preferred_element_type=F32).astype(BF16)

    def reduce_near(t, left):
        s = todo_s[t]
        tile = jnp.dot(left[...], panels_t[todo_j[t]], preferred_element_type=F32)
        upper = todo_b[t] // pairs
        parts[s] = jnp.where((lane >= 64) == (upper == 1), tile, parts[s])

    def steps(i, _):
        t = 2 * i
        reduce_near(t, l0)
        couple(t + 2, c0)
        reduce_own(t + 1, c1, l1)
        reduce_near(t + 1, l1)
        couple(t + 3, c1)
        reduce_own(t + 2, c0, l0)
        return 0

    lax.fori_loop(0, (n + 1) // 2, steps, 0)
    tiles[...] = parts[0:tiles.shape[0]].astype(tiles.dtype)


def place_kernel(near, counts, tiles, out, both, s_sem, r_sem):
    r, c = lax.axis_index("row"), lax.axis_index("col")
    blks, slots = near.shape
    pairs = blks // 2
    per = blks + 1
    half = out.shape[1]
    other = 1 - c
    barrier = pltpu.get_barrier_semaphore()
    pl.semaphore_signal(barrier, inc=1, device_id=(r, other), device_id_type=MESH)
    pl.semaphore_wait(barrier, 1)
    copy = pltpu.make_async_remote_copy(
        src_ref=tiles.at[:, pl.ds(pl.multiple_of(half * other, half), half)], dst_ref=both.at[c],
        send_sem=s_sem, recv_sem=r_sem, device_id=(r, other), device_id_type=MESH)
    copy.start()
    both[c] = tiles[:, pl.ds(pl.multiple_of(half * c, half), half)]
    copy.wait()
    first_block = r * blks
    for b in range(blks):
        up = b // pairs

        def one(k):
            j = near[b, k] - first_block + blks
            near_at = jnp.clip((j - b) // 2, 0, per - 1)
            tile = both[j % 2, (b % pairs) * per + near_at].astype(F32)
            tile = tile[:, 64 * up:64 * up + 64]
            return jnp.where(k < counts[b], tile, 0.0)

        for k in range(0, slots, 2):
            out[b, :, 64 * k:64 * k + 128] = jnp.concatenate([one(k), one(k + 1)], axis=1)


def on_device(rows, basis, positions, seglen, radius, neighbours, counts):
    blks, half, unk = basis.shape
    pairs = blks // 2
    per = blks + 1
    full = 2 * half
    slots = neighbours.shape[1]
    dma = pltpu.SemaphoreType.DMA
    own_p, halo_p, own_g, halo_g = pl.pallas_call(
        functools.partial(gather_kernel, rows),
        out_shape=(
            jax.ShapeDtypeStruct((2, pairs, full, unk), BF16),
            jax.ShapeDtypeStruct((2, pairs, full, unk), BF16),
            jax.ShapeDtypeStruct((2, 4 * pairs, unk), F32),
            jax.ShapeDtypeStruct((2, 4 * pairs, unk), F32),
        ),
        in_specs=[VMEM] * 4,
        out_specs=(VMEM,) * 4,
        scratch_shapes=[pltpu.VMEM((2, pairs, half, unk), BF16), dma, dma((2,)), dma((2,)), dma((2,)),
                        dma((2,)), dma((2,)), dma((2,)), dma],
        compiler_params=pltpu.CompilerParams(
            collective_id=0, has_side_effects=True, vmem_limit_bytes=24 << 20),
    )(basis, positions, seglen, radius)

    me = jnp.stack([lax.axis_index("row") * blks, lax.axis_index("col")]).astype(jnp.int32)
    tiles = pl.pallas_call(
        tile_kernel,
        out_shape=jax.ShapeDtypeStruct((pairs * per, full, 128), BF16),
        in_specs=[SMEM] * 3 + [VMEM] * 4,
        out_specs=VMEM,
        scratch_shapes=[
            pltpu.SMEM((blks * per,), jnp.int32),
            pltpu.SMEM((blks * slots + 8,), jnp.int32),
            pltpu.SMEM((blks * slots + 8,), jnp.int32),
            pltpu.SMEM((blks * slots + 8,), jnp.int32),
            pltpu.VMEM((blks, unk, 32), BF16),
            pltpu.VMEM((3 * pairs, 32, unk), BF16),
            pltpu.VMEM((3 * pairs, unk, 128), BF16),
            pltpu.VMEM((unk, unk), BF16),
            pltpu.VMEM((unk, unk), BF16),
            pltpu.VMEM((full, unk), BF16),
            pltpu.VMEM((full, unk), BF16),
            pltpu.VMEM((pairs * per + 1, full, 128), F32),
        ],
        compiler_params=pltpu.CompilerParams(vmem_limit_bytes=40 << 20),
    )(neighbours, counts, me, own_p, halo_p, own_g, halo_g)

    return pl.pallas_call(
        place_kernel,
        out_shape=jax.ShapeDtypeStruct((blks, half, 64 * slots), F32),
        in_specs=[SMEM] * 2 + [VMEM],
        out_specs=VMEM,
        scratch_shapes=[pltpu.VMEM((2, pairs * per, half, 128), BF16),
                        dma, dma],
        compiler_params=pltpu.CompilerParams(
            collective_id=1, has_side_effects=True, vmem_limit_bytes=24 << 20),
    )(neighbours, counts, tiles)


def solution(mesh):
    placed = (
        P("row", "col", None),
        P("row", None, None),
        P("row", None),
        P("row", None),
        P("row", None),
        P("row"),
    )
    return jax.shard_map(
        functools.partial(on_device, mesh.shape["row"]),
        mesh=mesh, in_specs=placed, out_specs=P("row", "col", None), check_vma=False
    )
```
